32 devices in a mesh: grp: 2 (over y), src: 4 (over z), snk: 4 (over x, core).
Axes of the slice: x: 2, y: 2, z: 4, core: 2. Of those that a mesh axis runs over, the one named last changes fastest.
Arguments:
- solutions: bfloat16 [8, 4, 2, 4, 64, 3, 128], P(('grp', 'src'), None, None, None, 'snk'), parts along dimension 0, may hold values from -6 to 6
- eigvecs: bfloat16 [8, 2, 64, 3, 512], P(('grp', 'snk')), parts along dimension 0, may hold values from -0.3125 to 0.3125
- momenta: int32 [8, 3], replicated, may hold values from -2 to 2
- ordering: int32 [512], replicated, may hold values from 0 to 511, each once
Outputs:
- peramb: bfloat16 [8, 4, 2, 512, 4, 128], P(('grp', 'snk'), 'src'), parts along dimension 0
- correlator: float32 [8, 4, 2, 8], P(('grp', 'snk'), 'src'), parts along dimension 0
The draws below stay inside these ranges and needn't reach their ends.
There are 2 independent parts, one for each index of `grp`. The reference program is written for one: setup_inputs(seed, part) draws one part's arguments, and reference() takes and returns one part's arrays. A program takes and returns all parts, laid end to end along the dimension named above; an argument that names none is the same for every part. Nothing has to cross between parts.
Inputs may be any that keep to these rules, and one draw needn't show every extreme that they name: `momenta`: components in units of 2 pi / 64; the third (z) has no effect on the window. `ordering`: each eigenvector index once.
All inputs are finite; a program needn't handle non-finite values.
Results may differ from the reference program's by a relative error of at most 0.0034.
Values may be sent and summed in bfloat16 or wider, within the bound.
A program may use at most 64 MiB of HBM per device.

```python
import math
import jax
import jax.numpy as jnp
from jax import lax

NEV = 512
DILUTION_COUNT = 128
WINDOW_SITES = 64
LAT = 64
MOMS = 8
NB = 32
SOURCE_TIMES = 4
SINK_TIMES = 4


def with_ends(values, stream_key, smallest, largest):
    shape = values.shape
    spot = [jax.random.randint(jax.random.fold_in(stream_key, axis), (), 0, shape[axis]) for axis in range(len(shape))]
    values = values.at[tuple(spot)].set(smallest)
    longest = shape.index(max(shape))
    spot[longest] = (spot[longest] + 1) % shape[longest]
    return values.at[tuple(spot)].set(largest)


def steps_of(rng, dims, cuts, low, largest):
    def one(axis_at, shards_of):
        steps = jax.random.uniform(jax.random.fold_in(jax.random.fold_in(rng, 6), axis_at), (shards_of,), jnp.float32, low / len(cuts), largest / len(cuts))
        return jnp.repeat(jnp.exp(steps), dims[axis_at] // shards_of).reshape((-1,) + (1,) * (len(dims) - axis_at - 1))

    level = one(*cuts[0])
    for cut in cuts[1:]:
        level = level * one(*cut)
    return level


def noise(rng, extent, scale, reach, pieces=(), kind=jnp.bfloat16):
    result = jax.random.normal(rng, extent, jnp.float32) * scale
    if len(pieces) > 0:
        result = steps_of(rng, extent, pieces, -0.22, 0.18) * result
    return jnp.clip(result, min=-reach, max=reach).astype(kind)


def setup_inputs(seed: int = 0, part: int = 0) -> dict:
    keys = jax.random.split(jax.random.key(seed), 5)
    own_keys = jax.random.split(jax.random.fold_in(keys[4], part), 5)
    solutions = noise(own_keys[0], (SOURCE_TIMES, SINK_TIMES, 2, 4, WINDOW_SITES, 3, DILUTION_COUNT), 1.0, 6.0, ((0, 4), (4, 4)))
    eigvecs = noise(own_keys[1], (SINK_TIMES, 2, WINDOW_SITES, 3, NEV), (6 * WINDOW_SITES) ** -0.5, 0.3125, ((0, 4),))
    momenta = with_ends(jax.random.randint(keys[2], (MOMS, 3), -2, 3), jax.random.fold_in(keys[2], 1), -2, 2).astype(jnp.int32)
    ordering = jax.random.permutation(keys[3], NEV).astype(jnp.int32)
    return dict(solutions=solutions, eigvecs=eigvecs, momenta=momenta, ordering=ordering)


PRECISE = lax.Precision.HIGHEST
SPIN_SIGNS = (1.0, 1.0, -1.0, -1.0)


def einsum_full(form, *operands):
    return jnp.einsum(form, *[item.astype(jnp.float32) for item in operands], precision=PRECISE)


def phase_tables(momenta):
    lattice_site_index = jnp.arange(WINDOW_SITES, dtype=jnp.int32)
    coord_x = (lattice_site_index % LAT).astype(jnp.float32)
    coord_y = ((lattice_site_index // LAT) % LAT).astype(jnp.float32)
    coord_z = (lattice_site_index // (LAT * LAT)).astype(jnp.float32)
    momentum_f = momenta.astype(jnp.float32)
    phase_angle = (2.0 * math.pi / LAT) * (momentum_f[:, 0:1] * coord_x[None, :] + momentum_f[:, 1:2] * coord_y[None, :] + momentum_f[:, 2:3] * coord_z[None, :])
    return jnp.cos(phase_angle), jnp.sin(phase_angle)


def block_onehot(ordering):
    block_ids = jnp.arange(NB, dtype=jnp.int32)
    return (ordering[:, None] // (NEV // NB) == block_ids[None, :]).astype(jnp.bfloat16)


def elementals_from(factors, phase_cos, phase_sine_part):
    fac_real, fac_imag = factors[0], factors[1]
    pair_real = einsum_full('xce,xcb->xeb', fac_real, fac_real) + einsum_full('xce,xcb->xeb', fac_imag, fac_imag)
    pairing_imaginary = einsum_full('xce,xcb->xeb', fac_real, fac_imag) - einsum_full('xce,xcb->xeb', fac_imag, fac_real)
    elemental_real = einsum_full('px,xeb->peb', phase_cos, pair_real) + einsum_full('px,xeb->peb', phase_sine_part, pairing_imaginary)
    elem_imag = einsum_full('px,xeb->peb', phase_cos, pairing_imaginary) - einsum_full('px,xeb->peb', phase_sine_part, pair_real)
    return jnp.stack([elemental_real, elem_imag])


def source_elementals(eigen, onehot, phase_cos, phase_sine_part):
    factors = einsum_full('rxck,kb->rxcb', eigen, onehot)
    return elementals_from(factors, phase_cos, phase_sine_part)


def sink_side(eigen, solution, phase_cos, phase_sine_part, elementals):
    eig_real, eig_imag = eigen[0], eigen[1]
    sol_real, sol_imag = solution[0], solution[1]
    tau_real = einsum_full('xck,axcd->kad', eig_real, sol_real) + einsum_full('xck,axcd->kad', eig_imag, sol_imag)
    tau_imag = einsum_full('xck,axcd->kad', eig_real, sol_imag) - einsum_full('xck,axcd->kad', eig_imag, sol_real)
    peramb = jnp.stack([tau_real, tau_imag]).astype(jnp.bfloat16)
    smear_real = einsum_full('xck,kad->axcd', eig_real, peramb[0]) - einsum_full('xck,kad->axcd', eig_imag, peramb[1])
    smear_imag = einsum_full('xck,kad->axcd', eig_real, peramb[1]) + einsum_full('xck,kad->axcd', eig_imag, peramb[0])
    smear_real = smear_real.reshape(4, WINDOW_SITES, 3, 4, NB)
    smear_imag = smear_imag.reshape(4, WINDOW_SITES, 3, 4, NB)
    spin_sign = jnp.array(SPIN_SIGNS, dtype=jnp.float32)
    loop_real = einsum_full('a,axcsb,axcse->xbe', spin_sign, smear_real, smear_real) + einsum_full('a,axcsb,axcse->xbe', spin_sign, smear_imag, smear_imag)
    loop_imag = einsum_full('a,axcsb,axcse->xbe', spin_sign, smear_real, smear_imag) - einsum_full('a,axcsb,axcse->xbe', spin_sign, smear_imag, smear_real)
    sink_real = einsum_full('px,xbe->pbe', phase_cos, loop_real) - einsum_full('px,xbe->pbe', phase_sine_part, loop_imag)
    sink_imag = einsum_full('px,xbe->pbe', phase_cos, loop_imag) + einsum_full('px,xbe->pbe', phase_sine_part, loop_real)
    src_real, src_imag = elementals[0], elementals[1]
    corr_real = einsum_full('pbe,peb->p', sink_real, src_real) - einsum_full('pbe,peb->p', sink_imag, src_imag)
    corr_imag = einsum_full('pbe,peb->p', sink_real, src_imag) + einsum_full('pbe,peb->p', sink_imag, src_real)
    return peramb, jnp.stack([corr_real, corr_imag]) * (1.0 / (WINDOW_SITES * NB))


def reference(solutions, eigvecs, momenta, ordering):
    phase_cos, phase_sine_part = phase_tables(momenta)
    onehot = block_onehot(ordering)
    all_elementals = lax.map(lambda eigen: source_elementals(eigen, onehot, phase_cos, phase_sine_part), eigvecs)

    def per_sink(sink_time):
        eigen = eigvecs[sink_time]

        def per_source(source_time):
            return sink_side(eigen, solutions[source_time, sink_time], phase_cos, phase_sine_part, all_elementals[source_time])

        return lax.map(per_source, jnp.arange(SOURCE_TIMES, dtype=jnp.int32))

    peramb, correlator = lax.map(per_sink, jnp.arange(SINK_TIMES, dtype=jnp.int32))
    return peramb, correlator
```

```python
import functools
import math

import jax
import jax.numpy as jnp
import numpy as np
from jax import lax
from jax.experimental import pallas as pl
from jax.experimental.pallas import tpu as pltpu
from jax.sharding import PartitionSpec as P

LAT = 64
NB = 32
SPIN_SIGNS = (1.0, 1.0, -1.0, -1.0)
EXACT = lax.Precision.HIGHEST
MESH = pl.DeviceIdType.MESH


def site_coordinates(peers, rows, colours, local):
    table = np.zeros((8, peers, rows), np.int32)
    for owner in range(peers):
        for colour in range(colours):
            site = owner * local + np.arange(local)
            here = slice(colour * local, (colour + 1) * local)
            table[0, owner, here] = site % LAT
            table[1, owner, here] = site // LAT % LAT
            table[2, owner, here] = site // (LAT * LAT)
    table = table.reshape(8, peers * rows)
    return np.concatenate([table, table], axis=1)


def split(values):
    high = values.astype(jnp.bfloat16).astype(jnp.float32)
    return high, values - high


def kernel(
    dims, momenta_ref, ordering_ref, coords_ref, eig_hbm, sol_hbm, peramb_ref, corr_ref,
    eig, eig_t, sol, pairs, fac_own, fac_got, table, weights,
    eig_sem, sol_sem, send_sem, recv_sem, fac_send, fac_recv,
):
    peers, spins, rows, local, colours, nev, dil, moms, direct, scale = dims
    total = peers * rows
    me = lax.axis_index("snk")
    source = lax.axis_index("src")

    if direct:
        eig_copies = [
            pltpu.make_async_copy(
                eig_hbm.at[:, c, j],
                eig.at[:, j, pl.ds(c * local, local)],
                eig_sem.at[j * colours + c],
            )
            for j in range(peers)
            for c in range(colours)
        ]
    else:
        eig_copies = [pltpu.make_async_copy(eig_hbm, eig, eig_sem.at[0])]
    own_copies = [
        pltpu.make_async_copy(sol_hbm.at[me, :, a], sol.at[a, :, me], sol_sem.at[a])
        for a in range(spins)
    ]
    for copy in eig_copies + own_copies:
        copy.start()

    barrier = pltpu.get_barrier_semaphore()
    for d in range(1, peers):
        other = lax.rem(me + d, peers)
        pl.semaphore_signal(barrier, inc=1, device_id={"snk": other}, device_id_type=MESH)
    pl.semaphore_wait(barrier, peers - 1)

    sends = []
    for a in range(spins):
        for d in range(1, peers):
            other = lax.rem(me + d, peers)
            copy = pltpu.make_async_remote_copy(
                src_ref=sol_hbm.at[other, :, a],
                dst_ref=sol.at[a, :, me],
                send_sem=send_sem.at[a, d],
                recv_sem=recv_sem.at[a, d],
                device_id={"snk": other},
                device_id_type=MESH,
            )
            copy.start()
            sends.append(copy)

    for copy in eig_copies:
        copy.wait()
    vectors = eig[...].reshape(2 * total, nev)
    block_of = lax.div(ordering_ref[...], jnp.int32(nev // NB))
    onehot = (block_of == lax.broadcasted_iota(jnp.int32, (NB, nev), 0)).astype(jnp.bfloat16)
    fac_own[...] = lax.dot_general(
        onehot, vectors, (((1,), (1,)), ((), ())), preferred_element_type=jnp.float32
    )

    fac_sends = []
    for d in range(1, peers):
        other = lax.rem(me + d, peers)
        fac_sends.append(
            pltpu.make_async_remote_copy(
                src_ref=fac_own,
                dst_ref=fac_got,
                send_sem=fac_send.at[d],
                recv_sem=fac_recv,
                device_id={"snk": other},
                device_id_type=MESH,
            )
        )

    @pl.when(me == source)
    def _():
        for copy in fac_sends:
            copy.start()

    eig_t[...] = vectors.astype(jnp.float32).T.astype(jnp.bfloat16)

    mom = [jnp.zeros((moms, 2 * total), jnp.int32) for _ in range(3)]
    which = lax.broadcasted_iota(jnp.int32, (moms, 2 * total), 0)
    for i in range(3):
        for p in range(moms):
            mom[i] = jnp.where(which == p, momenta_ref[p, i], mom[i])
    turns = sum(mom[i] * coords_ref[i : i + 1, :] for i in range(3))
    turns = jnp.bitwise_and(turns + LAT // 2, LAT - 1) - LAT // 2
    angle = turns.astype(jnp.float32) * (2.0 * math.pi / LAT)
    phases = jnp.concatenate([jnp.cos(angle), jnp.sin(angle)], axis=0)

    def smear(a):
        own_copies[a].wait()
        for copy in sends[a * (peers - 1) : (a + 1) * (peers - 1)]:
            copy.wait_recv()
        s_real = sol[a, 0].reshape(total, dil)
        s_imag = sol[a, 1].reshape(total, dil)
        right = jnp.concatenate(
            [
                jnp.concatenate([s_real, s_imag], axis=1),
                jnp.concatenate([s_imag, -s_real], axis=1),
            ],
            axis=0,
        )
        projected = jnp.dot(eig_t[...], right, preferred_element_type=jnp.float32)
        pairs[pl.ds(a, nev, stride=spins), :] = projected[:, :dil]
        pairs[pl.ds(nev * spins + a, nev, stride=spins), :] = projected[:, dil:]
        full = jnp.dot(
            eig[...].reshape(2 * total, nev),
            projected.astype(jnp.bfloat16),
            preferred_element_type=jnp.float32,
        )
        real = full[:total, :dil] - full[total:, dil:]
        imag = full[:total, dil:] + full[total:, :dil]
        return jnp.concatenate([real, imag], axis=1).T

    def correlate(a, smeared):
        high, low = split(smeared)
        high, low = high.astype(jnp.bfloat16), low.astype(jnp.bfloat16)
        part = jnp.zeros((2 * total, total), jnp.float32)
        for sigma in range(dil // NB):
            r, i = sigma * NB, dil + sigma * NB
            right = jnp.concatenate(
                [
                    high[r : r + NB], high[i : i + NB],
                    low[r : r + NB], low[i : i + NB],
                    high[r : r + NB], high[i : i + NB],
                ],
                axis=0,
            )
            g = jnp.dot(table[...], right, preferred_element_type=jnp.float32)
            part = part + g * g
        if a == 0:
            weights[...] = part * SPIN_SIGNS[a]
        elif SPIN_SIGNS[a] > 0:
            weights[...] += part
        else:
            weights[...] -= part

    first = smear(0)

    @pl.when(me != source)
    def _():
        fac_sends[0].wait_recv()

    @pl.when(me == source)
    def _():
        fac_got[...] = fac_own[...]

    got = fac_got[...]
    sign = jnp.where(lax.broadcasted_iota(jnp.int32, got.shape, 1) < total, 1.0, -1.0)
    swapped = pltpu.roll(got, total, 1)
    high, low = split(jnp.concatenate([got * sign, swapped], axis=0))
    table[...] = jnp.concatenate([high, high, low], axis=0).T.astype(jnp.bfloat16)

    correlate(0, first)
    for a in range(1, spins):
        correlate(a, smear(a))
    peramb_ref[...] = pairs[...].astype(jnp.bfloat16)

    summed = lax.dot_general(
        phases, weights[...], (((1,), (0,)), ((), ())),
        precision=EXACT, preferred_element_type=jnp.float32,
    )
    at_cos, at_sin = phases[:moms, :total], phases[moms:, :total]
    sum_cos, sum_sin = summed[:moms], summed[moms:]
    real = jnp.sum(at_cos * sum_cos + at_sin * sum_sin, axis=1, keepdims=True)
    imag = jnp.sum(at_sin * sum_cos - at_cos * sum_sin, axis=1, keepdims=True)
    square = (moms, moms)
    eye = lax.broadcasted_iota(jnp.int32, square, 0) == lax.broadcasted_iota(jnp.int32, square, 1)
    out = [
        jnp.sum(jnp.where(eye, column, 0.0), axis=0, keepdims=True) * scale
        for column in (real, imag)
    ]
    corr_ref[...] = jnp.concatenate(out, axis=0)

    for copy in sends:
        copy.wait_send()

    @pl.when(me == source)
    def _():
        for copy in fac_sends:
            copy.wait_send()


def body(peers, solutions, eigvecs, momenta, ordering):
    _, times, _, spins, local, colours, dil = solutions.shape
    sites, nev = eigvecs.shape[2], eigvecs.shape[4]
    moms = momenta.shape[0]
    used = colours * local
    rows = -(-used // 16) * 16
    direct = local % 16 == 0
    total = peers * rows

    sol = jnp.transpose(solutions[0], (0, 1, 2, 4, 3, 5)).reshape(times, 2, spins, used, dil)
    eig = jnp.transpose(eigvecs[0], (0, 2, 1, 3)).reshape(2, colours, peers, local, nev)
    if not direct:
        pad = ((0, 0), (0, 0), (0, 0), (0, rows - used), (0, 0))
        sol = jnp.pad(sol, pad)
        eig = jnp.transpose(eig, (0, 2, 1, 3, 4)).reshape(2, peers, used, nev)
        eig = jnp.pad(eig, pad[1:])
    coords = jnp.asarray(site_coordinates(peers, rows, colours, local))
    scale = 1.0 / (sites * NB)

    vmem = pl.BlockSpec(memory_space=pltpu.VMEM)
    dims = (peers, spins, rows, local, colours, nev, dil, moms, direct, scale)
    peramb, corr = pl.pallas_call(
        functools.partial(kernel, dims),
        out_shape=(
            jax.ShapeDtypeStruct((2 * nev * spins, dil), jnp.bfloat16),
            jax.ShapeDtypeStruct((2, moms), jnp.float32),
        ),
        in_specs=[
            pl.BlockSpec(memory_space=pltpu.SMEM),
            vmem,
            vmem,
            pl.BlockSpec(memory_space=pl.ANY),
            pl.BlockSpec(memory_space=pl.ANY),
        ],
        out_specs=(vmem, vmem),
        scratch_shapes=[
            pltpu.VMEM((2, peers, rows, nev), jnp.bfloat16),
            pltpu.VMEM((nev, 2 * total), jnp.bfloat16),
            pltpu.VMEM((spins, 2, peers, rows, dil), jnp.bfloat16),
            pltpu.VMEM((2 * nev * spins, dil), jnp.float32),
            pltpu.VMEM((NB, 2 * total), jnp.float32),
            pltpu.VMEM((NB, 2 * total), jnp.float32),
            pltpu.VMEM((2 * total, 6 * NB), jnp.bfloat16),
            pltpu.VMEM((2 * total, total), jnp.float32),
            pltpu.SemaphoreType.DMA((peers * colours,)),
            pltpu.SemaphoreType.DMA((spins,)),
            pltpu.SemaphoreType.DMA((spins, peers)),
            pltpu.SemaphoreType.DMA((spins, peers)),
            pltpu.SemaphoreType.DMA((peers,)),
            pltpu.SemaphoreType.DMA,
        ],
        compiler_params=pltpu.CompilerParams(
            collective_id=0, has_side_effects=True, vmem_limit_bytes=40 * 1024 * 1024
        ),
    )(momenta, ordering.reshape(1, nev), coords, eig, sol)
    return peramb.reshape(1, 1, 2, nev, spins, dil), corr.reshape(1, 1, 2, moms)


def solution(mesh):
    return jax.shard_map(
        functools.partial(body, mesh.shape["snk"]),
        mesh=mesh,
        in_specs=(
            P(("grp", "src"), None, None, None, "snk", None, None),
            P(("grp", "snk"), None, None, None, None),
            P(),
            P(),
        ),
        out_specs=(
            P(("grp", "snk"), "src", None, None, None, None),
            P(("grp", "snk"), "src", None, None),
        ),
        check_vma=False,
    )
```

```python
import functools
import math

import jax
import jax.numpy as jnp
from jax import lax
from jax.experimental import pallas as pl
from jax.experimental.pallas import tpu as pltpu
from jax.sharding import PartitionSpec as P

LAT = 64
NB = 32
SPIN_SIGNS = (1.0, 1.0, -1.0, -1.0)
EXACT = lax.Precision.HIGHEST
MESH = pl.DeviceIdType.MESH


def coordinates(peers, rows, local):
    total = peers * rows
    lane = lax.broadcasted_iota(jnp.int32, (1, 2 * total), 1)
    lane = jnp.where(lane >= total, lane - total, lane)
    owner = sum((lane >= j * rows).astype(jnp.int32) for j in range(1, peers))
    site = owner * local + lax.rem(lane - owner * rows, jnp.int32(local))
    x = lax.rem(site, jnp.int32(LAT))
    y = lax.rem(lax.div(site, jnp.int32(LAT)), jnp.int32(LAT))
    return x, y, lax.div(site, jnp.int32(LAT * LAT))


def split(values):
    high = values.astype(jnp.bfloat16).astype(jnp.float32)
    return high, values - high


def kernel(
    dims, momenta_hbm, ordering_hbm, eig_hbm, sol_hbm, peramb_ref, corr_ref,
    momenta_ref, ordering_ref, eig, eig_t, sol, pairs, fac_own, fac_got, table, weights,
    small_sem, eig_sem, sol_sem, send_sem, recv_sem, fac_send, fac_recv,
):
    peers, spins, rows, local, colours, nev, dil, moms, direct, scale = dims
    total = peers * rows
    me = lax.axis_index("snk")
    source = lax.axis_index("src")

    if direct:
        eig_copies = [
            pltpu.make_async_copy(
                eig_hbm.at[:, c, j],
                eig.at[:, j, pl.ds(c * local, local)],
                eig_sem.at[j * colours + c],
            )
            for j in range(peers)
            for c in range(colours)
        ]
    else:
        eig_copies = [pltpu.make_async_copy(eig_hbm, eig, eig_sem.at[0])]
    own_copies = [
        pltpu.make_async_copy(sol_hbm.at[me, :, a], sol.at[a, :, me], sol_sem.at[a])
        for a in range(spins)
    ]
    small_copies = [
        pltpu.make_async_copy(momenta_hbm, momenta_ref, small_sem.at[0]),
        pltpu.make_async_copy(ordering_hbm, ordering_ref, small_sem.at[1]),
    ]
    for copy in small_copies + eig_copies + own_copies:
        copy.start()

    barrier = pltpu.get_barrier_semaphore()
    for d in range(1, peers):
        other = lax.rem(me + d, peers)
        pl.semaphore_signal(barrier, inc=1, device_id={"snk": other}, device_id_type=MESH)
    pl.semaphore_wait(barrier, peers - 1)

    sends = []
    for a in range(spins):
        for d in range(1, peers):
            other = lax.rem(me + d, peers)
            copy = pltpu.make_async_remote_copy(
                src_ref=sol_hbm.at[other, :, a],
                dst_ref=sol.at[a, :, me],
                send_sem=send_sem.at[a, d],
                recv_sem=recv_sem.at[a, d],
                device_id={"snk": other},
                device_id_type=MESH,
            )
            copy.start()
            sends.append(copy)

    for copy in small_copies + eig_copies:
        copy.wait()
    vectors = eig[...].reshape(2 * total, nev)
    block_of = lax.div(ordering_ref[...], jnp.int32(nev // NB))
    onehot = (block_of == lax.broadcasted_iota(jnp.int32, (NB, nev), 0)).astype(jnp.bfloat16)
    fac_own[...] = lax.dot_general(
        onehot, vectors, (((1,), (1,)), ((), ())), preferred_element_type=jnp.float32
    )

    fac_sends = []
    for d in range(1, peers):
        other = lax.rem(me + d, peers)
        fac_sends.append(
            pltpu.make_async_remote_copy(
                src_ref=fac_own,
                dst_ref=fac_got,
                send_sem=fac_send.at[d],
                recv_sem=fac_recv,
                device_id={"snk": other},
                device_id_type=MESH,
            )
        )

    @pl.when(me == source)
    def _():
        for copy in fac_sends:
            copy.start()

    eig_t[...] = vectors.astype(jnp.float32).T.astype(jnp.bfloat16)

    square = (moms, moms)
    eye = lax.broadcasted_iota(jnp.int32, square, 0) == lax.broadcasted_iota(jnp.int32, square, 1)
    turns = jnp.zeros((moms, 2 * total), jnp.int32)
    for i, place in enumerate(coordinates(peers, rows, local)):
        column = jnp.sum(jnp.where(eye, momenta_ref[i : i + 1, :], 0), axis=1, keepdims=True)
        turns = turns + column * place
    turns = jnp.bitwise_and(turns + LAT // 2, LAT - 1) - LAT // 2
    angle = turns.astype(jnp.float32) * (2.0 * math.pi / LAT)
    phases = jnp.concatenate([jnp.cos(angle), jnp.sin(angle)], axis=0)

    def smear(a):
        own_copies[a].wait()
        for copy in sends[a * (peers - 1) : (a + 1) * (peers - 1)]:
            copy.wait_recv()
        s_real = sol[a, 0].reshape(total, dil)
        s_imag = sol[a, 1].reshape(total, dil)
        right = jnp.concatenate(
            [
                jnp.concatenate([s_real, s_imag], axis=1),
                jnp.concatenate([s_imag, -s_real], axis=1),
            ],
            axis=0,
        )
        projected = jnp.dot(eig_t[...], right, preferred_element_type=jnp.float32)
        pairs[pl.ds(a, nev, stride=spins), :] = projected[:, :dil]
        pairs[pl.ds(nev * spins + a, nev, stride=spins), :] = projected[:, dil:]
        full = jnp.dot(
            eig[...].reshape(2 * total, nev),
            projected.astype(jnp.bfloat16),
            preferred_element_type=jnp.float32,
        )
        real = full[:total, :dil] - full[total:, dil:]
        imag = full[:total, dil:] + full[total:, :dil]
        return jnp.concatenate([real, imag], axis=1).T

    def correlate(a, smeared):
        high, low = split(smeared)
        high, low = high.astype(jnp.bfloat16), low.astype(jnp.bfloat16)
        part = jnp.zeros((2 * total, total), jnp.float32)
        for sigma in range(dil // NB):
            r, i = sigma * NB, dil + sigma * NB
            right = jnp.concatenate(
                [
                    high[r : r + NB], high[i : i + NB],
                    low[r : r + NB], low[i : i + NB],
                    high[r : r + NB], high[i : i + NB],
                ],
                axis=0,
            )
            g = jnp.dot(table[...], right, preferred_element_type=jnp.float32)
            part = part + g * g
        if a == 0:
            weights[...] = part * SPIN_SIGNS[a]
        elif SPIN_SIGNS[a] > 0:
            weights[...] += part
        else:
            weights[...] -= part

    first = smear(0)

    @pl.when(me != source)
    def _():
        fac_sends[0].wait_recv()

    @pl.when(me == source)
    def _():
        fac_got[...] = fac_own[...]

    got = fac_got[...]
    sign = jnp.where(lax.broadcasted_iota(jnp.int32, got.shape, 1) < total, 1.0, -1.0)
    swapped = pltpu.roll(got, total, 1)
    high, low = split(jnp.concatenate([got * sign, swapped], axis=0))
    table[...] = jnp.concatenate([high, high, low], axis=0).T.astype(jnp.bfloat16)

    correlate(0, first)
    for a in range(1, spins):
        correlate(a, smear(a))
    peramb_ref[...] = pairs[...].astype(jnp.bfloat16)

    summed = lax.dot_general(
        phases, weights[...], (((1,), (0,)), ((), ())),
        precision=EXACT, preferred_element_type=jnp.float32,
    )
    at_cos, at_sin = phases[:moms, :total], phases[moms:, :total]
    sum_cos, sum_sin = summed[:moms], summed[moms:]
    real = jnp.sum(at_cos * sum_cos + at_sin * sum_sin, axis=1, keepdims=True)
    imag = jnp.sum(at_sin * sum_cos - at_cos * sum_sin, axis=1, keepdims=True)
    out = [
        jnp.sum(jnp.where(eye, column, 0.0), axis=0, keepdims=True) * scale
        for column in (real, imag)
    ]
    corr_ref[...] = jnp.concatenate(out, axis=0)

    for copy in sends:
        copy.wait_send()

    @pl.when(me == source)
    def _():
        for copy in fac_sends:
            copy.wait_send()


def body(peers, solutions, eigvecs, momenta, ordering):
    _, times, _, spins, local, colours, dil = solutions.shape
    sites, nev = eigvecs.shape[2], eigvecs.shape[4]
    moms = momenta.shape[0]
    used = colours * local
    rows = -(-used // 16) * 16
    direct = local % 16 == 0
    total = peers * rows

    sol = jnp.transpose(solutions[0], (0, 1, 2, 4, 3, 5)).reshape(times, 2, spins, used, dil)
    eig = jnp.transpose(eigvecs[0], (0, 2, 1, 3)).reshape(2, colours, peers, local, nev)
    if not direct:
        pad = ((0, 0), (0, 0), (0, 0), (0, rows - used), (0, 0))
        sol = jnp.pad(sol, pad)
        eig = jnp.transpose(eig, (0, 2, 1, 3, 4)).reshape(2, peers, used, nev)
        eig = jnp.pad(eig, pad[1:])
    scale = 1.0 / (sites * NB)

    operands = (momenta.T, ordering.reshape(1, nev), eig, sol)
    vmem = pl.BlockSpec(memory_space=pltpu.VMEM)
    dims = (peers, spins, rows, local, colours, nev, dil, moms, direct, scale)
    peramb, corr = pl.pallas_call(
        functools.partial(kernel, dims),
        out_shape=(
            jax.ShapeDtypeStruct((2 * nev * spins, dil), jnp.bfloat16),
            jax.ShapeDtypeStruct((2, moms), jnp.float32),
        ),
        in_specs=[pl.BlockSpec(memory_space=pltpu.HBM)] * 4,
        out_specs=(vmem, vmem),
        scratch_shapes=[
            pltpu.VMEM((3, moms), jnp.int32),
            pltpu.VMEM((1, nev), jnp.int32),
            pltpu.VMEM((2, peers, rows, nev), jnp.bfloat16),
            pltpu.VMEM((nev, 2 * total), jnp.bfloat16),
            pltpu.VMEM((spins, 2, peers, rows, dil), jnp.bfloat16),
            pltpu.VMEM((2 * nev * spins, dil), jnp.float32),
            pltpu.VMEM((NB, 2 * total), jnp.float32),
            pltpu.VMEM((NB, 2 * total), jnp.float32),
            pltpu.VMEM((2 * total, 6 * NB), jnp.bfloat16),
            pltpu.VMEM((2 * total, total), jnp.float32),
            pltpu.SemaphoreType.DMA((2,)),
            pltpu.SemaphoreType.DMA((peers * colours,)),
            pltpu.SemaphoreType.DMA((spins,)),
            pltpu.SemaphoreType.DMA((spins, peers)),
            pltpu.SemaphoreType.DMA((spins, peers)),
            pltpu.SemaphoreType.DMA((peers,)),
            pltpu.SemaphoreType.DMA,
        ],
        compiler_params=pltpu.CompilerParams(
            collective_id=0, has_side_effects=True, vmem_limit_bytes=40 * 1024 * 1024
        ),
    )(*(pltpu.with_memory_space_constraint(v, pltpu.HBM) for v in operands))
    return peramb.reshape(1, 1, 2, nev, spins, dil), corr.reshape(1, 1, 2, moms)


def solution(mesh):
    return jax.shard_map(
        functools.partial(body, mesh.shape["snk"]),
        mesh=mesh,
        in_specs=(
            P(("grp", "src"), None, None, None, "snk", None, None),
            P(("grp", "snk"), None, None, None, None),
            P(),
            P(),
        ),
        out_specs=(
            P(("grp", "snk"), "src", None, None, None, None),
            P(("grp", "snk"), "src", None, None),
        ),
        check_vma=False,
    )
```

```python
import functools
import math

import jax
import jax.numpy as jnp
from jax import lax
from jax.experimental import pallas as pl
from jax.experimental.pallas import tpu as pltpu
from jax.sharding import PartitionSpec as P

LAT = 64
NB = 32
AHEAD = 3
SPIN_SIGNS = (1.0, 1.0, -1.0, -1.0)
EXACT = lax.Precision.HIGHEST
MESH = pl.DeviceIdType.MESH


def coordinates(peers, rows, local):
    total = peers * rows
    lane = lax.broadcasted_iota(jnp.int32, (1, 2 * total), 1)
    lane = jnp.where(lane >= total, lane - total, lane)
    owner = sum((lane >= j * rows).astype(jnp.int32) for j in range(1, peers))
    site = owner * local + lax.rem(lane - owner * rows, jnp.int32(local))
    x = lax.rem(site, jnp.int32(LAT))
    y = lax.rem(lax.div(site, jnp.int32(LAT)), jnp.int32(LAT))
    return x, y, lax.div(site, jnp.int32(LAT * LAT))


def split(values):
    high = values.astype(jnp.bfloat16).astype(jnp.float32)
    return high, values - high


def kernel(
    dims, momenta_hbm, ordering_hbm, eig_hbm, sol_hbm, peramb_ref, corr_ref,
    momenta_ref, ordering_ref, eig, eig_t, sol, pairs, fac_own, fac_got, table, weights,
    small_sem, eig_sem, sol_sem, send_sem, recv_sem, fac_send, fac_recv,
):
    peers, spins, rows, local, colours, nev, dil, moms, direct, scale = dims
    total = peers * rows
    me = lax.axis_index("snk")
    source = lax.axis_index("src")

    if direct:
        eig_copies = [
            pltpu.make_async_copy(
                eig_hbm.at[:, c, j],
                eig.at[:, j, pl.ds(c * local, local)],
                eig_sem.at[j * colours + c],
            )
            for j in range(peers)
            for c in range(colours)
        ]
    else:
        eig_copies = [pltpu.make_async_copy(eig_hbm, eig, eig_sem.at[0])]
    own_copies = [
        pltpu.make_async_copy(sol_hbm.at[me, :, a], sol.at[a, :, me], sol_sem.at[a])
        for a in range(spins)
    ]
    small_copies = [
        pltpu.make_async_copy(momenta_hbm, momenta_ref, small_sem.at[0]),
        pltpu.make_async_copy(ordering_hbm, ordering_ref, small_sem.at[1]),
    ]
    for copy in small_copies + eig_copies + own_copies:
        copy.start()

    barrier = pltpu.get_barrier_semaphore()
    for d in range(1, peers):
        other = lax.rem(me + d, peers)
        pl.semaphore_signal(barrier, inc=1, device_id={"snk": other}, device_id_type=MESH)
    pl.semaphore_wait(barrier, peers - 1)

    sends = []
    for a in range(spins):
        for d in range(1, peers):
            other = lax.rem(me + d, peers)
            copy = pltpu.make_async_remote_copy(
                src_ref=sol_hbm.at[other, :, a],
                dst_ref=sol.at[a, :, me],
                send_sem=send_sem.at[a, d],
                recv_sem=recv_sem.at[a, d],
                device_id={"snk": other},
                device_id_type=MESH,
            )
            sends.append(copy)

    def spin_sends(a):
        return sends[a * (peers - 1) : (a + 1) * (peers - 1)]

    for a in range(min(AHEAD, spins)):
        for copy in spin_sends(a):
            copy.start()

    for copy in small_copies + eig_copies:
        copy.wait()
    vectors = eig[...].reshape(2 * total, nev)
    block_of = lax.div(ordering_ref[...], jnp.int32(nev // NB))
    onehot = (block_of == lax.broadcasted_iota(jnp.int32, (NB, nev), 0)).astype(jnp.bfloat16)
    fac_own[...] = lax.dot_general(
        onehot, vectors, (((1,), (1,)), ((), ())), preferred_element_type=jnp.float32
    )

    fac_sends = []
    for d in range(1, peers):
        other = lax.rem(me + d, peers)
        fac_sends.append(
            pltpu.make_async_remote_copy(
                src_ref=fac_own,
                dst_ref=fac_got,
                send_sem=fac_send.at[d],
                recv_sem=fac_recv,
                device_id={"snk": other},
                device_id_type=MESH,
            )
        )

    @pl.when(me == source)
    def _():
        for copy in fac_sends:
            copy.start()

    eig_t[...] = vectors.astype(jnp.float32).T.astype(jnp.bfloat16)

    square = (moms, moms)
    eye = lax.broadcasted_iota(jnp.int32, square, 0) == lax.broadcasted_iota(jnp.int32, square, 1)
    turns = jnp.zeros((moms, 2 * total), jnp.int32)
    for i, place in enumerate(coordinates(peers, rows, local)):
        column = jnp.sum(jnp.where(eye, momenta_ref[i : i + 1, :], 0), axis=1, keepdims=True)
        turns = turns + column * place
    turns = jnp.bitwise_and(turns + LAT // 2, LAT - 1) - LAT // 2
    angle = turns.astype(jnp.float32) * (2.0 * math.pi / LAT)
    phases = jnp.concatenate([jnp.cos(angle), jnp.sin(angle)], axis=0)

    def smear(a):
        own_copies[a].wait()
        for copy in spin_sends(a):
            copy.wait_recv()
        for copy in spin_sends(a):
            copy.wait_send()
        if a + AHEAD < spins:
            for copy in spin_sends(a + AHEAD):
                copy.start()
        s_real = sol[a, 0].reshape(total, dil)
        s_imag = sol[a, 1].reshape(total, dil)
        right = jnp.concatenate(
            [
                jnp.concatenate([s_real, s_imag], axis=1),
                jnp.concatenate([s_imag, -s_real], axis=1),
            ],
            axis=0,
        )
        projected = jnp.dot(eig_t[...], right, preferred_element_type=jnp.float32)
        pairs[pl.ds(a, nev, stride=spins), :] = projected[:, :dil]
        pairs[pl.ds(nev * spins + a, nev, stride=spins), :] = projected[:, dil:]
        full = jnp.dot(
            eig[...].reshape(2 * total, nev),
            projected.astype(jnp.bfloat16),
            preferred_element_type=jnp.float32,
        )
        real = full[:total, :dil] - full[total:, dil:]
        imag = full[:total, dil:] + full[total:, :dil]
        return jnp.concatenate([real, imag], axis=1).T

    def correlate(a, smeared):
        high, low = split(smeared)
        high, low = high.astype(jnp.bfloat16), low.astype(jnp.bfloat16)
        part = jnp.zeros((2 * total, total), jnp.float32)
        for sigma in range(dil // NB):
            r, i = sigma * NB, dil + sigma * NB
            right = jnp.concatenate(
                [
                    high[r : r + NB], high[i : i + NB],
                    low[r : r + NB], low[i : i + NB],
                    high[r : r + NB], high[i : i + NB],
                ],
                axis=0,
            )
            g = jnp.dot(table[...], right, preferred_element_type=jnp.float32)
            part = part + g * g
        if a == 0:
            weights[...] = part * SPIN_SIGNS[a]
        elif SPIN_SIGNS[a] > 0:
            weights[...] += part
        else:
            weights[...] -= part

    first = smear(0)

    @pl.when(me != source)
    def _():
        fac_sends[0].wait_recv()

    @pl.when(me == source)
    def _():
        fac_got[...] = fac_own[...]

    got = fac_got[...]
    sign = jnp.where(lax.broadcasted_iota(jnp.int32, got.shape, 1) < total, 1.0, -1.0)
    swapped = pltpu.roll(got, total, 1)
    high, low = split(jnp.concatenate([got * sign, swapped], axis=0))
    table[...] = jnp.concatenate([high, high, low], axis=0).T.astype(jnp.bfloat16)

    correlate(0, first)
    for a in range(1, spins):
        correlate(a, smear(a))
    peramb_ref[...] = pairs[...].astype(jnp.bfloat16)

    summed = lax.dot_general(
        phases, weights[...], (((1,), (0,)), ((), ())),
        precision=EXACT, preferred_element_type=jnp.float32,
    )
    at_cos, at_sin = phases[:moms, :total], phases[moms:, :total]
    sum_cos, sum_sin = summed[:moms], summed[moms:]
    real = jnp.sum(at_cos * sum_cos + at_sin * sum_sin, axis=1, keepdims=True)
    imag = jnp.sum(at_sin * sum_cos - at_cos * sum_sin, axis=1, keepdims=True)
    out = [
        jnp.sum(jnp.where(eye, column, 0.0), axis=0, keepdims=True) * scale
        for column in (real, imag)
    ]
    corr_ref[...] = jnp.concatenate(out, axis=0)

    @pl.when(me == source)
    def _():
        for copy in fac_sends:
            copy.wait_send()


def write_out(peramb, corr, peramb_hbm, corr_hbm, sems):
    pieces = sems.shape[0] - 1
    depth = peramb.shape[0] // pieces
    copies = [
        pltpu.make_async_copy(
            peramb.at[pl.ds(i * depth, depth)], peramb_hbm.at[pl.ds(i * depth, depth)], sems.at[i]
        )
        for i in range(pieces)
    ]
    copies.append(pltpu.make_async_copy(corr, corr_hbm, sems.at[pieces]))
    for copy in copies:
        copy.start()
    for copy in copies:
        copy.wait()


def body(peers, solutions, eigvecs, momenta, ordering):
    _, times, _, spins, local, colours, dil = solutions.shape
    sites, nev = eigvecs.shape[2], eigvecs.shape[4]
    moms = momenta.shape[0]
    used = colours * local
    rows = -(-used // 16) * 16
    direct = local % 16 == 0
    total = peers * rows

    sol = jnp.transpose(solutions[0], (0, 1, 2, 4, 3, 5)).reshape(times, 2, spins, used, dil)
    eig = jnp.transpose(eigvecs[0], (0, 2, 1, 3)).reshape(2, colours, peers, local, nev)
    if not direct:
        pad = ((0, 0), (0, 0), (0, 0), (0, rows - used), (0, 0))
        sol = jnp.pad(sol, pad)
        eig = jnp.transpose(eig, (0, 2, 1, 3, 4)).reshape(2, peers, used, nev)
        eig = jnp.pad(eig, pad[1:])
    scale = 1.0 / (sites * NB)

    operands = (momenta.T, ordering.reshape(1, nev), eig, sol)
    vmem = pl.BlockSpec(memory_space=pltpu.VMEM)
    dims = (peers, spins, rows, local, colours, nev, dil, moms, direct, scale)
    peramb, corr = pl.pallas_call(
        functools.partial(kernel, dims),
        out_shape=(
            jax.ShapeDtypeStruct((2 * nev * spins, dil), jnp.bfloat16),
            jax.ShapeDtypeStruct((2, moms), jnp.float32),
        ),
        in_specs=[pl.BlockSpec(memory_space=pltpu.HBM)] * 4,
        out_specs=(vmem, vmem),
        scratch_shapes=[
            pltpu.VMEM((3, moms), jnp.int32),
            pltpu.VMEM((1, nev), jnp.int32),
            pltpu.VMEM((2, peers, rows, nev), jnp.bfloat16),
            pltpu.VMEM((nev, 2 * total), jnp.bfloat16),
            pltpu.VMEM((spins, 2, peers, rows, dil), jnp.bfloat16),
            pltpu.VMEM((2 * nev * spins, dil), jnp.float32),
            pltpu.VMEM((NB, 2 * total), jnp.float32),
            pltpu.VMEM((NB, 2 * total), jnp.float32),
            pltpu.VMEM((2 * total, 6 * NB), jnp.bfloat16),
            pltpu.VMEM((2 * total, total), jnp.float32),
            pltpu.SemaphoreType.DMA((2,)),
            pltpu.SemaphoreType.DMA((peers * colours,)),
            pltpu.SemaphoreType.DMA((spins,)),
            pltpu.SemaphoreType.DMA((spins, peers)),
            pltpu.SemaphoreType.DMA((spins, peers)),
            pltpu.SemaphoreType.DMA((peers,)),
            pltpu.SemaphoreType.DMA,
        ],
        compiler_params=pltpu.CompilerParams(
            collective_id=0, has_side_effects=True, vmem_limit_bytes=40 * 1024 * 1024
        ),
    )(*(pltpu.with_memory_space_constraint(v, pltpu.HBM) for v in operands))
    hbm = pl.BlockSpec(memory_space=pltpu.HBM)
    peramb, corr = pl.pallas_call(
        write_out,
        out_shape=(
            jax.ShapeDtypeStruct(peramb.shape, peramb.dtype),
            jax.ShapeDtypeStruct(corr.shape, corr.dtype),
        ),
        in_specs=[vmem, vmem],
        out_specs=(hbm, hbm),
        scratch_shapes=[pltpu.SemaphoreType.DMA((5,))],
    )(*(pltpu.with_memory_space_constraint(v, pltpu.VMEM) for v in (peramb, corr)))
    return peramb.reshape(1, 1, 2, nev, spins, dil), corr.reshape(1, 1, 2, moms)


def solution(mesh):
    return jax.shard_map(
        functools.partial(body, mesh.shape["snk"]),
        mesh=mesh,
        in_specs=(
            P(("grp", "src"), None, None, None, "snk", None, None),
            P(("grp", "snk"), None, None, None, None),
            P(),
            P(),
        ),
        out_specs=(
            P(("grp", "snk"), "src", None, None, None, None),
            P(("grp", "snk"), "src", None, None),
        ),
        check_vma=False,
    )
```
